32 devices in a mesh: rows: 8 (over z, x), cols: 4 (over y, core).
Axes of the slice: x: 2, y: 2, z: 4, core: 2. Of those that a mesh axis runs over, the one named last changes fastest.
Arguments:
- a_tiles: bfloat16 [2304, 7, 128, 128], P(('rows', 'cols')), may hold values from -0.5 to 0.5
- a_cols: int32 [2304, 7], P(('rows', 'cols')), may hold values from 0 to 103, as said below
- ap_slot: int32 [2304, 7, 2], P(('rows', 'cols')), may hold values from 0 to 3
- p_tiles: bfloat16 [2304, 2, 128, 128], P(('rows', 'cols')), may hold values from -0.5 to 0.5
- p_aggs: int32 [2304, 2], P(('rows', 'cols')), may hold values from 0 to 127, as said below
- z_slot: int32 [2304, 2, 4], P(('rows', 'cols')), may hold values from 0 to 15
- send_rows: int32 [32, 4, 8], P(('rows', 'cols')), may hold values from 0 to 71
Outputs:
- coarse: float32 [128, 16, 128, 128], P(('rows', 'cols'))
The draws below stay inside these ranges and needn't reach their ends.
Inputs may be any that keep to these rules, and one draw needn't show every extreme that they name: `a_cols`: values below 72 are rows of the same device; a value v above names row send_rows[e, q, w % 8] with w = v - 72, q = w // 8 and e the fine row's neighbour in direction q, which always exists. `p_aggs`: column 0 names a coarse row of the fine row's own device; column 1 a coarse row of a device with the same cols index whose rows index differs by at most one; of one device's fine rows at most 9 have column 1 on one neighbouring rows index, and exactly 9 for some device.
All inputs are finite; a program needn't handle non-finite values.
Results may differ from the reference program's by a relative error of at most 0.0041.
Values may be sent and summed in bfloat16 or wider, within the bound.
A program may use at most 192 MiB of HBM per device.

```python
import jax
import jax.numpy as jnp
from jax import lax

TILE = 128
A_TILES = 7
P_TILES = 2
AP_SLOTS = 4
COARSE_SLOTS = 16
SEND = 8
ROWS_DEV = 72
CR_DEV = 4
CAP = 9
FINE = 2304
COARSE = 128
N_ROWS = 8
N_COLS = 4
DEVICES = 32


def draw_a_cols(key, part):
    key = jax.random.fold_in(key, 11)
    local_key, score_key, place_key, use_key = jax.random.split(key, 4)
    local = jax.random.randint(local_key, (DEVICES, ROWS_DEV, A_TILES), 0, ROWS_DEV)
    device = jnp.arange(DEVICES)[:, None]
    row_index = device // N_COLS
    col_index = device % N_COLS
    valid = jnp.stack([row_index > 0, row_index < N_ROWS - 1, col_index > 0, col_index < N_COLS - 1], -1)
    row = jnp.arange(ROWS_DEV)[None, :]
    planted_dir = row // SEND
    hit = (planted_dir[..., None] == jnp.arange(4)) & valid
    planted = jnp.any(hit, -1) & (row < 4 * SEND)
    last_tile = jnp.where(planted, ROWS_DEV + row, local[:, :, 6])
    scores = jax.random.randint(score_key, (DEVICES, ROWS_DEV, 4), 0, 1 << 20) * 4 + jnp.arange(4)
    scores = jnp.where(valid, scores, -1)
    picked = jnp.argmax(scores, -1)
    placed = jax.random.randint(place_key, (DEVICES, ROWS_DEV), 0, SEND)
    remote = ROWS_DEV + picked * SEND + placed
    used = jax.random.randint(use_key, (DEVICES, ROWS_DEV), 0, 4) == 0
    fifth_tile = jnp.where(used, remote, local[:, :, 5])
    joined = jnp.concatenate([local[:, :, :5], fifth_tile[..., None], last_tile[..., None]], -1)
    return joined.reshape(FINE, A_TILES).astype(jnp.int32)


def permute_one(device_key, values):
    return jax.random.permutation(device_key, values)


def draw_p_aggs(key, part):
    key = jax.random.fold_in(key, 7)
    count_key, pick_key, mix_key, first_key, second_key = jax.random.split(key, 5)
    device = jnp.arange(DEVICES)
    row_index = device // N_COLS
    counts = jax.random.randint(count_key, (DEVICES, 2), (CAP + 1) // 2, CAP + 1)
    chosen = jax.random.randint(pick_key, (), 0, (N_ROWS - 1) * N_COLS)
    counts = counts.at[chosen, 1].set(CAP)
    lower_count = jnp.where(row_index > 0, counts[:, 0], 0)
    upper_count = jnp.where(row_index < N_ROWS - 1, counts[:, 1], 0)
    order = jnp.arange(ROWS_DEV)[None, :]
    moves = jnp.where(order < lower_count[:, None], -1, jnp.where(order < (lower_count + upper_count)[:, None], 1, 0))
    mixed = jax.vmap(permute_one)(jax.random.split(mix_key, DEVICES), moves)
    first_slot = jax.random.randint(first_key, (DEVICES, ROWS_DEV), 0, CR_DEV)
    second_slot = jax.random.randint(second_key, (DEVICES, ROWS_DEV), 0, CR_DEV)
    primary = device[:, None] * CR_DEV + first_slot
    secondary = ((row_index[:, None] + mixed) * N_COLS + (device % N_COLS)[:, None]) * CR_DEV + second_slot
    return jnp.stack([primary, secondary], -1).reshape(FINE, 2).astype(jnp.int32)


def place_ends(result, own_key, least, largest):
    longest = result.shape.index(max(result.shape))
    spots = []
    for shift in (0, 1):
        where = [jax.random.randint(jax.random.fold_in(own_key, axis), (), 0, length) for axis, length in enumerate(result.shape)]
        where[longest] = (where[longest] + shift) % result.shape[longest]
        spots.append(tuple(where))
    return result.at[spots[0]].set(least).at[spots[1]].set(largest)


def block_scale(key, extent, shards, low, top_value):
    level = 1.0
    for dim, blocks in shards:
        heights = jax.random.uniform(jax.random.fold_in(jax.random.fold_in(key, 6), dim), (blocks,), jnp.float32, low / len(shards), top_value / len(shards))
        level = level * jnp.repeat(jnp.exp(heights), extent[dim] // blocks).reshape((-1,) + (1,) * (len(extent) - 1 - dim))
    return level


def noise(key, extent, width, bound, cuts=(), dtype=jnp.bfloat16):
    values = width * jax.random.normal(key, extent, jnp.float32)
    if cuts:
        values = values * block_scale(key, extent, cuts, -0.22, 0.18)
    return jnp.clip(values, -bound, bound).astype(dtype)


def setup_inputs(seed: int = 0) -> dict:
    key_of = jax.random.split(jax.random.key(seed), 8)
    return {
        "a_tiles": noise(key_of[0], (FINE, A_TILES, TILE, TILE), TILE ** -0.5, 0.5, ((0, 32),)),
        "a_cols": draw_a_cols(jax.random.fold_in(key_of[7], 71), 0),
        "ap_slot": place_ends(jax.random.randint(key_of[2], (FINE, A_TILES, P_TILES), 0, AP_SLOTS), jax.random.fold_in(key_of[2], 1), 0, AP_SLOTS - 1).astype(jnp.int32),
        "p_tiles": noise(key_of[3], (FINE, P_TILES, TILE, TILE), TILE ** -0.5, 0.5, ((0, 32),)),
        "p_aggs": draw_p_aggs(jax.random.fold_in(key_of[7], 71), 0),
        "z_slot": place_ends(jax.random.randint(key_of[5], (FINE, P_TILES, AP_SLOTS), 0, COARSE_SLOTS), jax.random.fold_in(key_of[5], 1), 0, COARSE_SLOTS - 1).astype(jnp.int32),
        "send_rows": place_ends(jax.random.randint(key_of[6], (DEVICES, 4, SEND), 0, ROWS_DEV), jax.random.fold_in(key_of[6], 1), 0, ROWS_DEV - 1).astype(jnp.int32),
    }


def reference(a_tiles, a_cols, ap_slot, p_tiles, p_aggs, z_slot, send_rows):
    owner_device = (jnp.arange(FINE) // ROWS_DEV).astype(jnp.int32)
    is_local = a_cols < ROWS_DEV
    ghost_index = jnp.maximum(a_cols - ROWS_DEV, 0)
    direction = (ghost_index // SEND).astype(jnp.int32)
    position = (ghost_index % SEND).astype(jnp.int32)
    offsets = jnp.array([-N_COLS, N_COLS, -1, 1], jnp.int32)
    source = jnp.clip(owner_device[:, None] + offsets[direction], 0, DEVICES - 1).astype(jnp.int32)
    sent_row = send_rows[source, direction, position]
    fine_col = jnp.where(is_local, owner_device[:, None] * ROWS_DEV + a_cols, source * ROWS_DEV + sent_row).astype(jnp.int32)
    slot_range = jnp.arange(AP_SLOTS).astype(jnp.int32)

    def device_terms(carry, device_index):
        first_row = (device_index * ROWS_DEV).astype(jnp.int32)
        a_part = lax.dynamic_slice_in_dim(a_tiles, first_row, ROWS_DEV, 0).astype(jnp.float32)
        col_part = lax.dynamic_slice_in_dim(fine_col, first_row, ROWS_DEV, 0)
        slot_part = lax.dynamic_slice_in_dim(ap_slot, first_row, ROWS_DEV, 0)
        p_part = lax.dynamic_slice_in_dim(p_tiles, first_row, ROWS_DEV, 0).astype(jnp.float32)
        agg_part = lax.dynamic_slice_in_dim(p_aggs, first_row, ROWS_DEV, 0)
        zs_part = lax.dynamic_slice_in_dim(z_slot, first_row, ROWS_DEV, 0)
        gathered = p_tiles[col_part].astype(jnp.float32)
        product = jnp.einsum("rkab,rklbc->rklac", a_part, gathered)
        onehot = (slot_part[..., None] == slot_range).astype(jnp.float32)
        strip = jnp.einsum("rkls,rklac->rsac", onehot, product, precision=lax.Precision.HIGHEST).astype(jnp.bfloat16)
        partial_value = jnp.einsum("rjba,rsbc->rjsac", p_part, strip.astype(jnp.float32)).astype(jnp.bfloat16)
        target = (agg_part[:, :, None] * COARSE_SLOTS + zs_part).astype(jnp.int32)
        carry = carry.at[target.reshape(-1)].add(partial_value.astype(jnp.float32).reshape(-1, TILE, TILE))
        return carry, None

    start = jnp.zeros((COARSE * COARSE_SLOTS, TILE, TILE), jnp.float32)
    total, unused = lax.scan(device_terms, start, jnp.arange(DEVICES).astype(jnp.int32))
    return total.reshape(COARSE, COARSE_SLOTS, TILE, TILE)
```

```python
import math

import jax
import jax.numpy as jnp
from jax import lax
from jax.experimental import pallas as pl
from jax.experimental.pallas import tpu as pltpu
from jax.sharding import PartitionSpec as P

COARSE_SLOTS = 16
CR_DEV = 4
SMEM = pltpu.SMEM
VMEM = pltpu.VMEM
ANY = pl.ANY
VMEM_LIMIT = 56 * 1024 * 1024

COLS, SLOTS, AGG, MOVE, ZS = 0, 7, 21, 23, 24


def passed_along(block, axis, distance):
    devices = range(lax.axis_size(axis))
    route = [(i - distance, i) for i in devices if i - distance in devices]
    return lax.ppermute(block, axis, route)


def pick_kernel(capacity, table, send, p_ref, *refs):
    outs, (rows_out, up_out, down_out), sems = refs[:4], refs[4:7], refs[7]
    sends = send.shape[2]
    copies = []
    for q in range(4):
        for j in range(sends):
            copies.append(
                pltpu.make_async_copy(
                    p_ref.at[send[0, q, j]], outs[q].at[j], sems.at[q * sends + j]
                )
            )
    for c in copies:
        c.start()
    for m in range(2 * capacity):
        rows_out[m] = 0
    for m in range(capacity):
        for s in range(4):
            up_out[m, s] = -1
            down_out[m, s] = -1

    def step(i, counts):
        n_up, n_down = counts
        move = table[i, MOVE]

        @pl.when(move == 1)
        def _():
            rows_out[n_up] = i
            for s in range(4):
                up_out[n_up, s] = table[i, AGG + 1] * COARSE_SLOTS + table[i, ZS + 4 + s]

        @pl.when(move == -1)
        def _():
            rows_out[capacity + n_down] = i
            for s in range(4):
                down_out[n_down, s] = table[i, AGG + 1] * COARSE_SLOTS + table[i, ZS + 4 + s]

        return (
            n_up + (move == 1).astype(jnp.int32),
            n_down + (move == -1).astype(jnp.int32),
        )

    lax.fori_loop(0, table.shape[0], step, (jnp.int32(0), jnp.int32(0)))
    for c in copies:
        c.wait()


def load_all(p_ref, ghosts, pall, sems):
    rows_here = p_ref.shape[0]
    sends = ghosts[0].shape[0]
    copies = [pltpu.make_async_copy(p_ref, pall.at[pl.ds(0, rows_here)], sems.at[0])]
    for q in range(4):
        copies.append(
            pltpu.make_async_copy(
                ghosts[q], pall.at[pl.ds(rows_here + q * sends, sends)], sems.at[1 + q]
            )
        )
    return copies


def strips_of(a_row, table, i, pall, acc):
    acc[...] = jnp.zeros_like(acc)
    for k in range(7):
        v = table[i, COLS + k]
        wide = jnp.concatenate([pall[v, 0], pall[v, 1]], axis=1)
        product = jnp.dot(a_row[k], wide, preferred_element_type=jnp.float32)
        for l in range(2):
            s = table[i, SLOTS + 2 * k + l]
            acc[s] += product[:, 128 * l : 128 * (l + 1)]
    return jnp.concatenate([acc[s].astype(jnp.bfloat16) for s in range(4)], axis=1)


def fold(left, strip):
    return lax.dot_general(
        left, strip, (((0,), (0,)), ((), ())), preferred_element_type=jnp.float32
    )


def outbox_kernel(capacity, table, rows, a_ref, p_ref, g0, g1, g2, g3, up, down, pall, abuf, acc, sems):
    copies = load_all(p_ref, (g0, g1, g2, g3), pall, sems)
    for c in copies:
        c.start()
    arows = [
        pltpu.make_async_copy(a_ref.at[rows[m]], abuf.at[m], sems.at[5 + m])
        for m in range(2 * capacity)
    ]
    for c in arows:
        c.start()
    for c in copies + arows:
        c.wait()
    for side, out in enumerate((up, down)):

        def step(m, carry, side=side, out=out):
            i = rows[side * capacity + m]
            strip = strips_of(abuf.at[side * capacity + m], table, i, pall, acc)
            part = fold(pall[i, 1], strip)
            for s in range(4):
                out[m, s] = part[:, 128 * s : 128 * (s + 1)].astype(jnp.bfloat16)
            return carry

        lax.fori_loop(0, capacity, step, 0)


def main_kernel(table, a_ref, p_ref, g0, g1, g2, g3, out, pall, acc, sems):
    g = pl.program_id(0)
    block = a_ref.shape[0]

    @pl.when(g == 0)
    def _():
        copies = load_all(p_ref, (g0, g1, g2, g3), pall, sems)
        for c in copies:
            c.start()
        out[...] = jnp.zeros_like(out)
        for c in copies:
            c.wait()

    def step(b, carry):
        i = g * block + b
        strip = strips_of(a_ref.at[b], table, i, pall, acc)
        part = fold(pall[i, 0], strip)
        base = table[i, AGG] * COARSE_SLOTS
        for s in range(4):
            out[base + table[i, ZS + s]] += part[:, 128 * s : 128 * (s + 1)]

        @pl.when(table[i, MOVE] == 0)
        def _():
            part = fold(pall[i, 1], strip)
            base = table[i, AGG + 1] * COARSE_SLOTS
            for s in range(4):
                out[base + table[i, ZS + 4 + s]] += part[:, 128 * s : 128 * (s + 1)]

        return carry

    lax.fori_loop(0, block, step, 0)


def add_kernel(up_tags, down_tags, up, down, c_in, c_out):
    g = pl.program_id(0)
    c_out[...] = c_in[...]
    for tags, got in ((up_tags, up), (down_tags, down)):

        def step(m, carry, tags=tags, got=got):
            for s in range(4):
                t = tags[m, s]

                @pl.when((t >= 0) & (t // COARSE_SLOTS == g))
                def _():
                    c_out[0, t % COARSE_SLOTS] += got[m, s].astype(jnp.float32)

            return carry

        lax.fori_loop(0, got.shape[0], step, 0)


def local(a_tiles, a_cols, ap_slot, p_tiles, p_aggs, z_slot, send_rows):
    rows_here, _, tile, _ = a_tiles.shape
    sends = send_rows.shape[2]
    capacity = max(2, rows_here // 8)
    col_devices = lax.axis_size("cols")
    row_index = lax.axis_index("rows")
    move = p_aggs[:, 1:] // CR_DEV // col_devices - row_index
    table = jnp.concatenate(
        [
            a_cols,
            ap_slot.reshape(rows_here, 14),
            p_aggs % CR_DEV,
            move,
            z_slot.reshape(rows_here, 8),
        ],
        axis=1,
    )
    smem = pl.BlockSpec(memory_space=SMEM)
    anys = pl.BlockSpec(memory_space=ANY)
    vmem = pl.BlockSpec(memory_space=VMEM)
    ghost = jax.ShapeDtypeStruct((sends, 2, tile, tile), jnp.bfloat16)
    tags = jax.ShapeDtypeStruct((capacity, 4), jnp.int32)
    *sending, rows, up_tags, down_tags = pl.pallas_call(
        lambda *r: pick_kernel(capacity, *r),
        out_shape=[ghost] * 4 + [jax.ShapeDtypeStruct((2 * capacity,), jnp.int32), tags, tags],
        in_specs=[smem, smem, anys],
        out_specs=[anys] * 4 + [smem] * 3,
        scratch_shapes=[pltpu.SemaphoreType.DMA((4 * sends,))],
    )(table, send_rows, p_tiles)
    ghosts = [
        passed_along(sending[0], "rows", 1),
        passed_along(sending[1], "rows", -1),
        passed_along(sending[2], "cols", 1),
        passed_along(sending[3], "cols", -1),
    ]
    up_tags = passed_along(up_tags + 1, "rows", 1) - 1
    down_tags = passed_along(down_tags + 1, "rows", -1) - 1
    box = jax.ShapeDtypeStruct((capacity, 4, tile, tile), jnp.bfloat16)
    all_rows = rows_here + 4 * sends
    params = pltpu.CompilerParams(vmem_limit_bytes=VMEM_LIMIT)
    up, down = pl.pallas_call(
        lambda *r: outbox_kernel(capacity, *r),
        out_shape=[box, box],
        in_specs=[smem, smem] + [anys] * 6,
        out_specs=[vmem, vmem],
        scratch_shapes=[
            VMEM((all_rows, 2, tile, tile), jnp.bfloat16),
            VMEM((2 * capacity, 7, tile, tile), jnp.bfloat16),
            VMEM((4, tile, tile), jnp.float32),
            pltpu.SemaphoreType.DMA((5 + 2 * capacity,)),
        ],
        compiler_params=params,
    )(table, rows, a_tiles, p_tiles, *ghosts)
    up = passed_along(up, "rows", 1)
    down = passed_along(down, "rows", -1)
    block = math.gcd(rows_here, 8)
    tile_count = CR_DEV * COARSE_SLOTS
    coarse = pl.pallas_call(
        main_kernel,
        out_shape=jax.ShapeDtypeStruct((tile_count, tile, tile), jnp.float32),
        grid=(rows_here // block,),
        in_specs=[
            smem,
            pl.BlockSpec((block, 7, tile, tile), lambda g: (g, 0, 0, 0)),
        ]
        + [anys] * 5,
        out_specs=pl.BlockSpec((tile_count, tile, tile), lambda g: (0, 0, 0)),
        scratch_shapes=[
            VMEM((all_rows, 2, tile, tile), jnp.bfloat16),
            VMEM((4, tile, tile), jnp.float32),
            pltpu.SemaphoreType.DMA((5,)),
        ],
        compiler_params=params,
        cost_estimate=pl.CostEstimate(
            flops=2 * rows_here * 22 * tile**3, bytes_accessed=26_000_000, transcendentals=0
        ),
    )(table, a_tiles, p_tiles, *ghosts)
    coarse = coarse.reshape(CR_DEV, COARSE_SLOTS, tile, tile)
    part = pl.BlockSpec((1, COARSE_SLOTS, tile, tile), lambda g: (g, 0, 0, 0))
    whole = pl.BlockSpec((capacity, 4, tile, tile), lambda g: (0, 0, 0, 0))
    return pl.pallas_call(
        add_kernel,
        out_shape=jax.ShapeDtypeStruct(coarse.shape, jnp.float32),
        grid=(CR_DEV,),
        in_specs=[smem, smem, whole, whole, part],
        out_specs=part,
        compiler_params=params,
    )(up_tags, down_tags, up, down, coarse)


def solution(mesh):
    spec = P(("rows", "cols"))
    return jax.shard_map(
        local,
        mesh=mesh,
        in_specs=(spec,) * 7,
        out_specs=spec,
        check_vma=False,
    )
```

```python
import math

import jax
import jax.numpy as jnp
from jax import lax
from jax.experimental import pallas as pl
from jax.experimental.pallas import tpu as pltpu
from jax.sharding import PartitionSpec as P

COARSE_SLOTS = 16
CR_DEV = 4
TILES = CR_DEV * COARSE_SLOTS
SMEM = pltpu.SMEM
VMEM = pltpu.VMEM
ANY = pl.ANY
DMA = pltpu.SemaphoreType.DMA
MESH = pl.DeviceIdType.MESH
VMEM_LIMIT = 56 * 1024 * 1024
EARLY = 2
TOGETHER = 4

COLS, SLOTS, AGG, MOVE, ZS = 0, 7, 21, 23, 24


def passed_along(block, axis, distance):
    devices = range(lax.axis_size(axis))
    route = [(i - distance, i) for i in devices if i - distance in devices]
    return lax.ppermute(block, axis, route)


def directions():
    r, c = lax.axis_index("rows"), lax.axis_index("cols")
    nr, nc = lax.axis_size("rows"), lax.axis_size("cols")
    return [
        ((r + 1, c), r < nr - 1, r > 0),
        ((r - 1, c), r > 0, r < nr - 1),
        ((r, c + 1), c < nc - 1, c > 0),
        ((r, c - 1), c > 0, c < nc - 1),
    ]


def fold(left, strip):
    return lax.dot_general(
        left, strip, (((0,), (0,)), ((), ())), preferred_element_type=jnp.float32
    )


def front_kernel(
    capacity,
    table,
    send,
    a_ref,
    p_ref,
    table_ref,
    ghost_out,
    early_up,
    early_down,
    table_up,
    table_down,
    late_up,
    late_down,
    pall,
    abuf,
    stage,
    land,
    box_up,
    box_down,
    prod,
    rows,
    sems,
    send_sems,
    recv_sems,
):
    rows_here = p_ref.shape[0]
    sends = send.shape[2]
    dirs = directions()
    p_copy = pltpu.make_async_copy(p_ref, pall.at[pl.ds(0, rows_here)], sems.at[0])
    p_copy.start()
    barrier = pltpu.get_barrier_semaphore()
    for target, sending, _ in dirs:

        @pl.when(sending)
        def _(target=target):
            pl.semaphore_signal(barrier, inc=1, device_id=target, device_id_type=MESH)

    p_copy.wait()
    a_copy = pltpu.make_async_copy(a_ref, abuf, sems.at[1])
    a_copy.start()
    for q in range(4):

        def pick(j, carry, q=q):
            stage[q, j] = pall[send[0, q, j]]
            return carry

        lax.fori_loop(0, sends, pick, 0)
    peers = sum(sending.astype(jnp.int32) for _, sending, _ in dirs)
    pl.semaphore_wait(barrier, peers)

    def remote(n, source, place, q):
        return pltpu.make_async_remote_copy(
            src_ref=source,
            dst_ref=place,
            send_sem=send_sems.at[n],
            recv_sem=recv_sems.at[n],
            device_id=dirs[q][0],
            device_id_type=MESH,
        )

    moves = [
        (remote(q, stage.at[q], land.at[pl.ds(q * sends, sends)], q), q) for q in range(4)
    ] + [(remote(4, table_ref, table_up, 0), 0), (remote(5, table_ref, table_down, 1), 1)]

    def start(pairs):
        for copy, q in pairs:

            @pl.when(dirs[q][1])
            def _(copy=copy):
                copy.start()

    def finish(pairs):
        for copy, q in pairs:

            @pl.when(dirs[q][1])
            def _(copy=copy):
                copy.wait_send()

            @pl.when(dirs[q][2])
            def _(copy=copy):
                copy.wait_recv()

    start(moves)

    zero = jnp.int32(0)

    def scan(i, carry):
        n_up, n_down, found = carry
        move = table[i, MOVE]
        is_up, is_down = move == 1, move == -1
        found = tuple(
            jnp.where(
                is_up & (n_up == m) if m < capacity else is_down & (n_down == m - capacity),
                i,
                old,
            )
            for m, old in enumerate(found)
        )
        return n_up + is_up.astype(jnp.int32), n_down + is_down.astype(jnp.int32), found

    _, _, found = lax.fori_loop(0, rows_here, scan, (zero, zero, (zero,) * (2 * capacity)))
    for m, i in enumerate(found):
        rows[m] = i
    a_copy.wait()
    finish(moves)
    ghost_copy = pltpu.make_async_copy(land, ghost_out, sems.at[2])
    ghost_copy.start()
    pall[pl.ds(rows_here, 4 * sends)] = land[...]

    def products(m, places):
        strips = []
        lines = [rows[m], rows[capacity + m]]
        for side, i in enumerate(lines):
            for k in range(7):
                v = table[i, COLS + k]
                wide = jnp.concatenate([pall[v, 0], pall[v, 1]], axis=1)
                prod[side, k] = jnp.dot(abuf[i, k], wide, preferred_element_type=jnp.float32)
        for side, i in enumerate(lines):
            slots = [table[i, SLOTS + n] for n in range(14)]
            gains = [[(x == s).astype(jnp.float32) for s in range(4)] for x in slots]
            chunks = []
            for top in range(0, 128, 16):
                sums = [None] * 4
                for n in range(14):
                    k, l = n // 2, n % 2
                    value = prod[side, k, top : top + 16, 128 * l : 128 * (l + 1)]
                    for s in range(4):
                        term = value * gains[n][s]
                        sums[s] = term if n == 0 else sums[s] + term
                chunks.append(jnp.concatenate([x.astype(jnp.bfloat16) for x in sums], axis=1))
            strips.append(jnp.concatenate(chunks, axis=0))
        for side, i in enumerate(lines):
            part = fold(pall[i, 1], strips[side])
            out, place = places[side]
            for s in range(4):
                out[place, s] = part[:, 128 * s : 128 * (s + 1)].astype(jnp.bfloat16)

    def early_step(m, carry):
        products(m, ((box_up, m), (box_down, m)))
        return carry

    def late_step(m, carry):
        products(m, ((late_up, m - EARLY), (late_down, m - EARLY)))
        return carry

    lax.fori_loop(0, EARLY, early_step, 0)
    early = [(remote(6, box_up, early_up, 0), 0), (remote(7, box_down, early_down, 1), 1)]
    start(early)
    lax.fori_loop(EARLY, capacity, late_step, 0)
    ghost_copy.wait()
    finish(early)


def main_kernel(
    capacity, flags, table, table_up, table_down, a_ref, p_ref, ghosts, early_up, early_down,
    out, tags, pall, got, sems, *accs
):
    g = pl.program_id(0)
    block = a_ref.shape[0]
    rows_here = p_ref.shape[0]

    @pl.when(g == 0)
    def _():
        copies = [
            pltpu.make_async_copy(p_ref, pall.at[pl.ds(0, rows_here)], sems.at[0]),
            pltpu.make_async_copy(ghosts, pall.at[pl.ds(rows_here, ghosts.shape[0])], sems.at[1]),
            pltpu.make_async_copy(early_up, got.at[0], sems.at[2]),
            pltpu.make_async_copy(early_down, got.at[1], sems.at[3]),
        ]
        for c in copies:
            c.start()
        out[...] = jnp.zeros_like(out)
        for m in range(2 * capacity):
            tags[m, 0] = -1
        for side, (other, sign) in enumerate(((table_up, 1), (table_down, -1))):

            @pl.when(flags[side] == 1)
            def _(side=side, other=other, sign=sign):
                def scan(i, n):
                    hit = other[i, MOVE] == sign

                    @pl.when(hit)
                    def _():
                        tags[side * capacity + n, 0] = other[i, AGG + 1]
                        for s in range(4):
                            tags[side * capacity + n, 1 + s] = other[i, ZS + 4 + s]

                    return n + hit.astype(jnp.int32)

                lax.fori_loop(0, rows_here, scan, jnp.int32(0))

        for c in copies:
            c.wait()
        for side in range(2):
            for m in range(EARLY):
                a = tags[side * capacity + m, 0]

                @pl.when(a >= 0)
                def _(side=side, m=m, a=a):
                    for s in range(4):
                        t = a * COARSE_SLOTS + tags[side * capacity + m, 1 + s]
                        out[t] += got[side, m, s].astype(jnp.float32)

    def step(b, carry):
        first = b * TOGETHER
        lines = [g * block + first + n for n in range(TOGETHER)]
        for acc in accs:
            acc[...] = jnp.zeros_like(acc)
        for k in range(7):
            for n, i in enumerate(lines):
                v = table[i, COLS + k]
                wide = jnp.concatenate([pall[v, 0], pall[v, 1]], axis=1)
                product = jnp.dot(a_ref[first + n, k], wide, preferred_element_type=jnp.float32)
                for l in range(2):
                    accs[n][table[i, SLOTS + 2 * k + l]] += product[:, 128 * l : 128 * (l + 1)]
        for n, i in enumerate(lines):
            strip = jnp.concatenate([accs[n][s].astype(jnp.bfloat16) for s in range(4)], axis=1)
            for j in range(2):
                part = fold(pall[i, j], strip)
                base = table[i, AGG + j] * COARSE_SLOTS
                for s in range(4):
                    t = base + table[i, ZS + 4 * j + s]
                    if j:
                        t = jnp.where(table[i, MOVE] == 0, t, TILES)
                    out[t] += part[:, 128 * s : 128 * (s + 1)]
        return carry

    lax.fori_loop(0, block // TOGETHER, step, 0)


def add_kernel(capacity, tags, up, down, c_in, c_out):
    g = pl.program_id(0)
    c_out[0] = c_in[...]
    for side, got in ((0, up), (1, down)):

        def step(m, carry, side=side, got=got):
            line = side * capacity + EARLY + m

            @pl.when(tags[line, 0] == g)
            def _():
                for s in range(4):
                    c_out[0, tags[line, 1 + s]] += got[m, s].astype(jnp.float32)

            return carry

        lax.fori_loop(0, got.shape[0], step, 0)


def local(a_tiles, a_cols, ap_slot, p_tiles, p_aggs, z_slot, send_rows):
    rows_here, _, tile, _ = a_tiles.shape
    sends = send_rows.shape[2]
    capacity = max(2, rows_here // 8)
    late = capacity - EARLY
    col_devices = lax.axis_size("cols")
    row_index = lax.axis_index("rows")
    move = p_aggs[:, 1:] // CR_DEV // col_devices - row_index
    table = jnp.concatenate(
        [
            a_cols,
            ap_slot.reshape(rows_here, 14),
            p_aggs % CR_DEV,
            move,
            z_slot.reshape(rows_here, 8),
        ],
        axis=1,
    )
    flags = jnp.stack([row_index > 0, row_index < lax.axis_size("rows") - 1]).astype(jnp.int32)
    smem = pl.BlockSpec(memory_space=SMEM)
    anys = pl.BlockSpec(memory_space=ANY)
    vmem = pl.BlockSpec(memory_space=VMEM)
    bf16 = jnp.bfloat16
    all_rows = rows_here + 4 * sends

    def boxes(n):
        return jax.ShapeDtypeStruct((n, 4, tile, tile), bf16)

    table_shape = jax.ShapeDtypeStruct(table.shape, jnp.int32)
    ghosts, early_up, early_down, table_up, table_down, late_up, late_down = pl.pallas_call(
        lambda *r: front_kernel(capacity, *r),
        out_shape=[
            jax.ShapeDtypeStruct((4 * sends, 2, tile, tile), bf16),
            boxes(EARLY),
            boxes(EARLY),
            table_shape,
            table_shape,
            boxes(late),
            boxes(late),
        ],
        in_specs=[smem, smem] + [anys] * 3,
        out_specs=[anys] * 5 + [vmem] * 2,
        scratch_shapes=[
            VMEM((all_rows, 2, tile, tile), bf16),
            VMEM((rows_here, 7, tile, tile), bf16),
            VMEM((4, sends, 2, tile, tile), bf16),
            VMEM((4 * sends, 2, tile, tile), bf16),
            VMEM((EARLY, 4, tile, tile), bf16),
            VMEM((EARLY, 4, tile, tile), bf16),
            VMEM((2, 7, tile, 2 * tile), jnp.float32),
            SMEM((2 * capacity,), jnp.int32),
            DMA((3,)),
            DMA((8,)),
            DMA((8,)),
        ],
        compiler_params=pltpu.CompilerParams(
            vmem_limit_bytes=VMEM_LIMIT, collective_id=0, has_side_effects=True
        ),
        cost_estimate=pl.CostEstimate(
            flops=2 * capacity * 36 * tile**3, bytes_accessed=25_000_000, transcendentals=0
        ),
    )(table, send_rows, a_tiles, p_tiles, table)
    up = passed_along(late_up, "rows", 1)
    down = passed_along(late_down, "rows", -1)
    block = math.gcd(rows_here, 8)
    params = pltpu.CompilerParams(vmem_limit_bytes=VMEM_LIMIT)
    coarse, tags = pl.pallas_call(
        lambda *r: main_kernel(capacity, *r),
        out_shape=[
            jax.ShapeDtypeStruct((TILES + 1, tile, tile), jnp.float32),
            jax.ShapeDtypeStruct((2 * capacity, 5), jnp.int32),
        ],
        grid=(rows_here // block,),
        in_specs=[smem] * 4
        + [pl.BlockSpec((block, 7, tile, tile), lambda g: (g, 0, 0, 0))]
        + [anys] * 4,
        out_specs=[pl.BlockSpec((TILES + 1, tile, tile), lambda g: (0, 0, 0)), smem],
        scratch_shapes=[
            VMEM((all_rows, 2, tile, tile), bf16),
            VMEM((2, EARLY, 4, tile, tile), bf16),
            DMA((4,)),
        ]
        + [VMEM((4, tile, tile), jnp.float32)] * TOGETHER,
        compiler_params=params,
        cost_estimate=pl.CostEstimate(
            flops=2 * rows_here * 22 * tile**3, bytes_accessed=26_000_000, transcendentals=0
        ),
    )(flags, table, table_up, table_down, a_tiles, p_tiles, ghosts, early_up, early_down)
    whole = pl.BlockSpec((late, 4, tile, tile), lambda g: (0, 0, 0, 0))
    return pl.pallas_call(
        lambda *r: add_kernel(capacity, *r),
        out_shape=jax.ShapeDtypeStruct((CR_DEV, COARSE_SLOTS, tile, tile), jnp.float32),
        grid=(CR_DEV,),
        in_specs=[
            smem,
            whole,
            whole,
            pl.BlockSpec((COARSE_SLOTS, tile, tile), lambda g: (g, 0, 0)),
        ],
        out_specs=pl.BlockSpec((1, COARSE_SLOTS, tile, tile), lambda g: (g, 0, 0, 0)),
        compiler_params=params,
    )(tags, up, down, coarse)


def solution(mesh):
    spec = P(("rows", "cols"))
    return jax.shard_map(
        local,
        mesh=mesh,
        in_specs=(spec,) * 7,
        out_specs=spec,
        check_vma=False,
    )
```

```python
import math

import jax
import jax.numpy as jnp
from jax import lax
from jax.experimental import pallas as pl
from jax.experimental.pallas import tpu as pltpu
from jax.sharding import PartitionSpec as P

COARSE_SLOTS = 16
CR_DEV = 4
TILES = CR_DEV * COARSE_SLOTS
SMEM = pltpu.SMEM
VMEM = pltpu.VMEM
ANY = pl.ANY
DMA = pltpu.SemaphoreType.DMA
MESH = pl.DeviceIdType.MESH
VMEM_LIMIT = 56 * 1024 * 1024
MAIN_LIMIT = 32 * 1024 * 1024
ADD_LIMIT = 20 * 1024 * 1024
EARLY = 4
TOGETHER = 4


def passed_along(block, axis, distance):
    devices = range(lax.axis_size(axis))
    route = [(i - distance, i) for i in devices if i - distance in devices]
    return lax.ppermute(block, axis, route)


def directions():
    r, c = lax.axis_index("rows"), lax.axis_index("cols")
    nr, nc = lax.axis_size("rows"), lax.axis_size("cols")
    return [
        ((r + 1, c), r < nr - 1, r > 0),
        ((r - 1, c), r > 0, r < nr - 1),
        ((r, c + 1), c < nc - 1, c > 0),
        ((r, c - 1), c > 0, c < nc - 1),
    ]


def fold(left, strip):
    return lax.dot_general(
        left, strip, (((0,), (0,)), ((), ())), preferred_element_type=jnp.float32
    )


def front_kernel(
    capacity,
    cols,
    slot,
    aggs,
    send,
    a_ref,
    p_ref,
    aggs_ref,
    z_ref,
    ghost_out,
    early_up,
    early_down,
    aggs_up,
    aggs_down,
    z_up,
    z_down,
    late_up,
    late_down,
    pall,
    abuf,
    stage,
    land,
    box_up,
    box_down,
    prod,
    rows,
    sems,
    send_sems,
    recv_sems,
):
    rows_here = p_ref.shape[0]
    sends = send.shape[2]
    dirs = directions()
    p_copy = pltpu.make_async_copy(p_ref, pall.at[pl.ds(0, rows_here)], sems.at[0])
    p_copy.start()
    barrier = pltpu.get_barrier_semaphore()
    for target, sending, _ in dirs:

        @pl.when(sending)
        def _(target=target):
            pl.semaphore_signal(barrier, inc=1, device_id=target, device_id_type=MESH)

    p_copy.wait()
    a_copy = pltpu.make_async_copy(a_ref, abuf, sems.at[1])
    a_copy.start()
    peers = sum(sending.astype(jnp.int32) for _, sending, _ in dirs)
    pl.semaphore_wait(barrier, peers)

    def remote(n, source, place, q):
        return pltpu.make_async_remote_copy(
            src_ref=source,
            dst_ref=place,
            send_sem=send_sems.at[n],
            recv_sem=recv_sems.at[n],
            device_id=dirs[q][0],
            device_id_type=MESH,
        )

    moves = [
        (remote(q, stage.at[q], land.at[pl.ds(q * sends, sends)], q), q) for q in range(4)
    ] + [
        (remote(4, aggs_ref, aggs_up, 0), 0),
        (remote(5, aggs_ref, aggs_down, 1), 1),
        (remote(6, z_ref, z_up, 0), 0),
        (remote(7, z_ref, z_down, 1), 1),
    ]

    def start(pairs):
        for copy, q in pairs:

            @pl.when(dirs[q][1])
            def _(copy=copy):
                copy.start()

    def finish(pairs):
        for copy, q in pairs:

            @pl.when(dirs[q][1])
            def _(copy=copy):
                copy.wait_send()

            @pl.when(dirs[q][2])
            def _(copy=copy):
                copy.wait_recv()

    for q in range(4):

        def pick(j, carry, q=q):
            stage[q, j] = pall[send[0, q, j]]
            return carry

        lax.fori_loop(0, sends, pick, 0)
        start(moves[q : q + 1])
    start(moves[4:])

    row_index = lax.axis_index("rows")
    row_span = CR_DEV * lax.axis_size("cols")
    zero = jnp.int32(0)

    def scan(i, carry):
        n_up, n_down, found = carry
        move = lax.div(aggs[1, i], row_span) - row_index
        is_up, is_down = move == 1, move == -1
        found = tuple(
            jnp.where(
                is_up & (n_up == m) if m < capacity else is_down & (n_down == m - capacity),
                i,
                old,
            )
            for m, old in enumerate(found)
        )
        return n_up + is_up.astype(jnp.int32), n_down + is_down.astype(jnp.int32), found

    _, _, found = lax.fori_loop(0, rows_here, scan, (zero, zero, (zero,) * (2 * capacity)))
    for m, i in enumerate(found):
        rows[m] = i
    a_copy.wait()
    finish(moves)
    ghost_copy = pltpu.make_async_copy(land, ghost_out, sems.at[2])
    ghost_copy.start()
    pall[pl.ds(rows_here, 4 * sends)] = land[...]

    def products(m, places):
        strips = []
        lines = [rows[m], rows[capacity + m]]
        for side, i in enumerate(lines):
            for k in range(7):
                v = cols[k, i]
                wide = jnp.concatenate([pall[v, 0], pall[v, 1]], axis=1)
                prod[side, k] = jnp.dot(abuf[i, k], wide, preferred_element_type=jnp.float32)
        for side, i in enumerate(lines):
            slots = [slot[n // 2, n % 2, i] for n in range(14)]
            gains = [[(x == s).astype(jnp.float32) for s in range(4)] for x in slots]
            chunks = []
            for top in range(0, 128, 16):
                sums = [None] * 4
                for n in range(14):
                    k, l = n // 2, n % 2
                    value = prod[side, k, top : top + 16, 128 * l : 128 * (l + 1)]
                    for s in range(4):
                        term = value * gains[n][s]
                        sums[s] = term if n == 0 else sums[s] + term
                chunks.append(jnp.concatenate([x.astype(jnp.bfloat16) for x in sums], axis=1))
            strips.append(jnp.concatenate(chunks, axis=0))
        for side, i in enumerate(lines):
            part = fold(pall[i, 1], strips[side])
            out, place = places[side]
            for s in range(4):
                out[place, s] = part[:, 128 * s : 128 * (s + 1)].astype(jnp.bfloat16)

    def early_pairs(m):
        return [
            (remote(8 + 2 * m, box_up.at[m], early_up.at[m], 0), 0),
            (remote(9 + 2 * m, box_down.at[m], early_down.at[m], 1), 1),
        ]

    def early_step(m, carry):
        products(m, ((box_up, m), (box_down, m)))
        start(early_pairs(m))
        return carry

    def late_step(m, carry):
        products(m, ((late_up, m - EARLY), (late_down, m - EARLY)))
        return carry

    def early_end(m, carry):
        finish(early_pairs(m))
        return carry

    lax.fori_loop(0, EARLY, early_step, 0)
    lax.fori_loop(EARLY, capacity, late_step, 0)
    ghost_copy.wait()
    lax.fori_loop(0, EARLY, early_end, 0)


def main_kernel(
    capacity, cols, slot, aggs, z, aggs_up, aggs_down, z_up, z_down, a_ref, p_ref, ghosts,
    early_up, early_down, out, tags, pall, got, sems, *accs
):
    g = pl.program_id(0)
    block = a_ref.shape[0]
    rows_here = p_ref.shape[0]
    row_index = lax.axis_index("rows")
    row_span = CR_DEV * lax.axis_size("cols")

    @pl.when(g == 0)
    def _():
        copies = [
            pltpu.make_async_copy(p_ref, pall.at[pl.ds(0, rows_here)], sems.at[0]),
            pltpu.make_async_copy(ghosts, pall.at[pl.ds(rows_here, ghosts.shape[0])], sems.at[1]),
            pltpu.make_async_copy(early_up, got.at[0], sems.at[2]),
            pltpu.make_async_copy(early_down, got.at[1], sems.at[3]),
        ]
        for c in copies:
            c.start()
        out[...] = jnp.zeros_like(out)
        for m in range(2 * capacity):
            tags[m, 0] = -1
        received = (
            (aggs_up, z_up, row_index > 0),
            (aggs_down, z_down, row_index < lax.axis_size("rows") - 1),
        )
        for side, (other, other_z, there) in enumerate(received):

            @pl.when(there)
            def _(side=side, other=other, other_z=other_z):
                def scan(i, n):
                    a = other[1, i]
                    hit = lax.div(a, row_span) == row_index

                    @pl.when(hit)
                    def _():
                        tags[side * capacity + n, 0] = lax.rem(a, CR_DEV)
                        for s in range(4):
                            tags[side * capacity + n, 1 + s] = other_z[1, s, i]

                    return n + hit.astype(jnp.int32)

                lax.fori_loop(0, rows_here, scan, jnp.int32(0))

        for c in copies:
            c.wait()
        for side in range(2):
            for m in range(EARLY):
                a = tags[side * capacity + m, 0]

                @pl.when(a >= 0)
                def _(side=side, m=m, a=a):
                    for s in range(4):
                        t = a * COARSE_SLOTS + tags[side * capacity + m, 1 + s]
                        out[t] += got[side, m, s].astype(jnp.float32)

    def step(b, carry):
        first = b * TOGETHER
        lines = [g * block + first + n for n in range(TOGETHER)]
        for acc in accs:
            acc[...] = jnp.zeros_like(acc)
        for k in range(7):
            for n, i in enumerate(lines):
                v = cols[k, i]
                wide = jnp.concatenate([pall[v, 0], pall[v, 1]], axis=1)
                product = jnp.dot(a_ref[first + n, k], wide, preferred_element_type=jnp.float32)
                for l in range(2):
                    accs[n][slot[k, l, i]] += product[:, 128 * l : 128 * (l + 1)]
        for n, i in enumerate(lines):
            strip = jnp.concatenate([accs[n][s].astype(jnp.bfloat16) for s in range(4)], axis=1)
            for j in range(2):
                part = fold(pall[i, j], strip)
                base = lax.rem(aggs[j, i], CR_DEV) * COARSE_SLOTS
                here = lax.div(aggs[j, i], row_span) == row_index
                for s in range(4):
                    t = base + z[j, s, i]
                    if j:
                        t = jnp.where(here, t, TILES)
                    out[t] += part[:, 128 * s : 128 * (s + 1)]
        return carry

    lax.fori_loop(0, block // TOGETHER, step, 0)


def add_kernel(capacity, tags, up, down, c_in, c_out):
    g = pl.program_id(0)
    c_out[0] = c_in[...]
    for side, got in ((0, up), (1, down)):

        def step(m, carry, side=side, got=got):
            line = side * capacity + EARLY + m

            @pl.when(tags[line, 0] == g)
            def _():
                for s in range(4):
                    c_out[0, tags[line, 1 + s]] += got[m, s].astype(jnp.float32)

            return carry

        lax.fori_loop(0, got.shape[0], step, 0)


def local(a_tiles, a_cols, ap_slot, p_tiles, p_aggs, z_slot, send_rows):
    rows_here, _, tile, _ = a_tiles.shape
    a_cols, p_aggs = a_cols.T, p_aggs.T
    ap_slot, z_slot = ap_slot.transpose(1, 2, 0), z_slot.transpose(1, 2, 0)
    sends = send_rows.shape[2]
    capacity = max(2, rows_here // 8)
    late = capacity - EARLY
    smem = pl.BlockSpec(memory_space=SMEM)
    anys = pl.BlockSpec(memory_space=ANY)
    vmem = pl.BlockSpec(memory_space=VMEM)
    bf16 = jnp.bfloat16
    all_rows = rows_here + 4 * sends

    def boxes(n):
        return jax.ShapeDtypeStruct((n, 4, tile, tile), bf16)

    aggs_shape = jax.ShapeDtypeStruct(p_aggs.shape, jnp.int32)
    z_shape = jax.ShapeDtypeStruct(z_slot.shape, jnp.int32)
    ghosts, early_up, early_down, aggs_up, aggs_down, z_up, z_down, late_up, late_down = pl.pallas_call(
        lambda *r: front_kernel(capacity, *r),
        out_shape=[
            jax.ShapeDtypeStruct((4 * sends, 2, tile, tile), bf16),
            boxes(EARLY),
            boxes(EARLY),
            aggs_shape,
            aggs_shape,
            z_shape,
            z_shape,
            boxes(late),
            boxes(late),
        ],
        in_specs=[smem] * 4 + [anys] * 4,
        out_specs=[anys] * 7 + [vmem] * 2,
        scratch_shapes=[
            VMEM((all_rows, 2, tile, tile), bf16),
            VMEM((rows_here, 7, tile, tile), bf16),
            VMEM((4, sends, 2, tile, tile), bf16),
            VMEM((4 * sends, 2, tile, tile), bf16),
            VMEM((EARLY, 4, tile, tile), bf16),
            VMEM((EARLY, 4, tile, tile), bf16),
            VMEM((2, 7, tile, 2 * tile), jnp.float32),
            SMEM((2 * capacity,), jnp.int32),
            DMA((3,)),
            DMA((8 + 2 * EARLY,)),
            DMA((8 + 2 * EARLY,)),
        ],
        compiler_params=pltpu.CompilerParams(
            vmem_limit_bytes=VMEM_LIMIT, collective_id=0, has_side_effects=True
        ),
        cost_estimate=pl.CostEstimate(
            flops=2 * capacity * 36 * tile**3, bytes_accessed=25_000_000, transcendentals=0
        ),
    )(a_cols, ap_slot, p_aggs, send_rows, a_tiles, p_tiles, p_aggs, z_slot)
    up = passed_along(late_up, "rows", 1)
    down = passed_along(late_down, "rows", -1)
    block = math.gcd(rows_here, 8)
    coarse, tags = pl.pallas_call(
        lambda *r: main_kernel(capacity, *r),
        out_shape=[
            jax.ShapeDtypeStruct((TILES + 1, tile, tile), jnp.float32),
            jax.ShapeDtypeStruct((2 * capacity, 5), jnp.int32),
        ],
        grid=(rows_here // block,),
        in_specs=[smem] * 8
        + [pl.BlockSpec((block, 7, tile, tile), lambda g: (g, 0, 0, 0))]
        + [anys] * 4,
        out_specs=[pl.BlockSpec((TILES + 1, tile, tile), lambda g: (0, 0, 0)), smem],
        scratch_shapes=[
            VMEM((all_rows, 2, tile, tile), bf16),
            VMEM((2, EARLY, 4, tile, tile), bf16),
            DMA((4,)),
        ]
        + [VMEM((4, tile, tile), jnp.float32)] * TOGETHER,
        compiler_params=pltpu.CompilerParams(vmem_limit_bytes=MAIN_LIMIT),
        cost_estimate=pl.CostEstimate(
            flops=2 * rows_here * 22 * tile**3, bytes_accessed=26_000_000, transcendentals=0
        ),
    )(
        a_cols, ap_slot, p_aggs, z_slot, aggs_up, aggs_down, z_up, z_down,
        a_tiles, p_tiles, ghosts, early_up, early_down,
    )
    whole = pl.BlockSpec((late, 4, tile, tile), lambda g: (0, 0, 0, 0))
    return pl.pallas_call(
        lambda *r: add_kernel(capacity, *r),
        out_shape=jax.ShapeDtypeStruct((CR_DEV, COARSE_SLOTS, tile, tile), jnp.float32),
        grid=(CR_DEV,),
        in_specs=[
            smem,
            whole,
            whole,
            pl.BlockSpec((COARSE_SLOTS, tile, tile), lambda g: (g, 0, 0)),
        ],
        out_specs=pl.BlockSpec((1, COARSE_SLOTS, tile, tile), lambda g: (g, 0, 0, 0)),
        compiler_params=pltpu.CompilerParams(vmem_limit_bytes=ADD_LIMIT),
    )(tags, up, down, coarse)


def solution(mesh):
    spec = P(("rows", "cols"))
    return jax.shard_map(
        local,
        mesh=mesh,
        in_specs=(spec,) * 7,
        out_specs=spec,
        check_vma=False,
    )
```

```python
import math

import jax
import jax.numpy as jnp
from jax import lax
from jax.experimental import pallas as pl
from jax.experimental.pallas import tpu as pltpu
from jax.sharding import PartitionSpec as P

COARSE_SLOTS = 16
CR_DEV = 4
TILES = CR_DEV * COARSE_SLOTS
SMEM = pltpu.SMEM
VMEM = pltpu.VMEM
ANY = pl.ANY
DMA = pltpu.SemaphoreType.DMA
MESH = pl.DeviceIdType.MESH
VMEM_LIMIT = 56 * 1024 * 1024
MAIN_LIMIT = 56 * 1024 * 1024
ADD_LIMIT = 20 * 1024 * 1024
EARLY = 3
GROUP = 3
TOGETHER = 4


def passed_along(block, axis, distance):
    devices = range(lax.axis_size(axis))
    route = [(i - distance, i) for i in devices if i - distance in devices]
    return lax.ppermute(block, axis, route)


def directions():
    r, c = lax.axis_index("rows"), lax.axis_index("cols")
    nr, nc = lax.axis_size("rows"), lax.axis_size("cols")
    return [
        ((r + 1, c), r < nr - 1, r > 0),
        ((r - 1, c), r > 0, r < nr - 1),
        ((r, c + 1), c < nc - 1, c > 0),
        ((r, c - 1), c > 0, c < nc - 1),
    ]


def fold(left, strip):
    return lax.dot_general(
        left, strip, (((0,), (0,)), ((), ())), preferred_element_type=jnp.float32
    )


def front_kernel(
    capacity,
    cols,
    slot,
    aggs,
    send,
    a_ref,
    p_ref,
    aggs_ref,
    z_ref,
    ghost_out,
    early_up,
    early_down,
    aggs_up,
    aggs_down,
    z_up,
    z_down,
    late_up,
    late_down,
    pall,
    abuf,
    stage,
    land,
    box_up,
    box_down,
    prod,
    rows,
    sems,
    send_sems,
    recv_sems,
):
    rows_here = p_ref.shape[0]
    sends = send.shape[2]
    dirs = directions()
    p_copy = pltpu.make_async_copy(p_ref, pall.at[pl.ds(0, rows_here)], sems.at[0])
    p_copy.start()
    barrier = pltpu.get_barrier_semaphore()
    for target, sending, _ in dirs:

        @pl.when(sending)
        def _(target=target):
            pl.semaphore_signal(barrier, inc=1, device_id=target, device_id_type=MESH)

    p_copy.wait()
    a_copy = pltpu.make_async_copy(a_ref, abuf, sems.at[1])
    a_copy.start()
    peers = sum(sending.astype(jnp.int32) for _, sending, _ in dirs)
    pl.semaphore_wait(barrier, peers)

    def remote(n, source, place, q):
        return pltpu.make_async_remote_copy(
            src_ref=source,
            dst_ref=place,
            send_sem=send_sems.at[n],
            recv_sem=recv_sems.at[n],
            device_id=dirs[q][0],
            device_id_type=MESH,
        )

    moves = [
        (remote(q, stage.at[q], land.at[pl.ds(q * sends, sends)], q), q) for q in range(4)
    ] + [
        (remote(4, aggs_ref, aggs_up, 0), 0),
        (remote(5, aggs_ref, aggs_down, 1), 1),
        (remote(6, z_ref, z_up, 0), 0),
        (remote(7, z_ref, z_down, 1), 1),
    ]

    def start(pairs):
        for copy, q in pairs:

            @pl.when(dirs[q][1])
            def _(copy=copy):
                copy.start()

    def finish(pairs):
        for copy, q in pairs:

            @pl.when(dirs[q][1])
            def _(copy=copy):
                copy.wait_send()

            @pl.when(dirs[q][2])
            def _(copy=copy):
                copy.wait_recv()

    for q in range(4):

        def pick(j, carry, q=q):
            stage[q, j] = pall[send[0, q, j]]
            return carry

        lax.fori_loop(0, sends, pick, 0)
        start(moves[q : q + 1])
    start(moves[4:])

    row_index = lax.axis_index("rows")
    row_span = CR_DEV * lax.axis_size("cols")
    zero = jnp.int32(0)

    def scan(i, carry):
        n_up, n_down, found = carry
        move = lax.div(aggs[1, i], row_span) - row_index
        is_up, is_down = move == 1, move == -1
        found = tuple(
            jnp.where(
                is_up & (n_up == m) if m < capacity else is_down & (n_down == m - capacity),
                i,
                old,
            )
            for m, old in enumerate(found)
        )
        return n_up + is_up.astype(jnp.int32), n_down + is_down.astype(jnp.int32), found

    _, _, found = lax.fori_loop(0, rows_here, scan, (zero, zero, (zero,) * (2 * capacity)))
    for m, i in enumerate(found):
        rows[m] = i
    a_copy.wait()
    finish(moves)
    ghost_copy = pltpu.make_async_copy(land, ghost_out, sems.at[2])
    ghost_copy.start()
    pall[pl.ds(rows_here, 4 * sends)] = land[...]

    def products(places):
        strips = []
        lines = [line for line, _, _ in places]
        for side, i in enumerate(lines):
            for k in range(7):
                v = cols[k, i]
                wide = jnp.concatenate([pall[v, 0], pall[v, 1]], axis=1)
                prod[side, k] = jnp.dot(abuf[i, k], wide, preferred_element_type=jnp.float32)
        for side, i in enumerate(lines):
            slots = [slot[n // 2, n % 2, i] for n in range(14)]
            gains = [[(x == s).astype(jnp.float32) for s in range(4)] for x in slots]
            chunks = []
            for top in range(0, 128, 16):
                sums = [None] * 4
                for n in range(14):
                    k, l = n // 2, n % 2
                    value = prod[side, k, top : top + 16, 128 * l : 128 * (l + 1)]
                    for s in range(4):
                        term = value * gains[n][s]
                        sums[s] = term if n == 0 else sums[s] + term
                chunks.append(jnp.concatenate([x.astype(jnp.bfloat16) for x in sums], axis=1))
            strips.append(jnp.concatenate(chunks, axis=0))
        for side, i in enumerate(lines):
            part = fold(pall[i, 1], strips[side])
            _, out, place = places[side]
            for s in range(4):
                out[place, s] = part[:, 128 * s : 128 * (s + 1)].astype(jnp.bfloat16)

    def early_pairs(m):
        return [
            (remote(8 + 2 * m, box_up.at[m], early_up.at[m], 0), 0),
            (remote(9 + 2 * m, box_down.at[m], early_down.at[m], 1), 1),
        ]

    def group(first, size, up, down, skipped):
        places = []
        for n in range(size):
            m = first + n
            places.append((rows[m], up, m - skipped))
            places.append((rows[capacity + m], down, m - skipped))
        products(places)

    def late_step(n, carry):
        group(EARLY + n * GROUP, GROUP, late_up, late_down, EARLY)
        return carry

    def early_end(m, carry):
        finish(early_pairs(m))
        return carry

    group(0, EARLY, box_up, box_down, 0)
    for m in range(EARLY):
        start(early_pairs(m))
    steps, rest = divmod(capacity - EARLY, GROUP)
    lax.fori_loop(0, steps, late_step, 0)
    if rest:
        group(capacity - rest, rest, late_up, late_down, EARLY)
    ghost_copy.wait()
    lax.fori_loop(0, EARLY, early_end, 0)


def main_kernel(
    capacity, cols, slot, aggs, z, aggs_up, aggs_down, z_up, z_down, a_ref, p_ref, ghosts,
    early_up, early_down, out, tags, pall, got, sems, *accs
):
    g = pl.program_id(0)
    block = a_ref.shape[0]
    rows_here = p_ref.shape[0]
    row_index = lax.axis_index("rows")
    row_span = CR_DEV * lax.axis_size("cols")

    @pl.when(g == 0)
    def _():
        copies = [
            pltpu.make_async_copy(p_ref, pall.at[pl.ds(0, rows_here)], sems.at[0]),
            pltpu.make_async_copy(ghosts, pall.at[pl.ds(rows_here, ghosts.shape[0])], sems.at[1]),
            pltpu.make_async_copy(early_up, got.at[0], sems.at[2]),
            pltpu.make_async_copy(early_down, got.at[1], sems.at[3]),
        ]
        for c in copies:
            c.start()
        out[...] = jnp.zeros_like(out)
        for m in range(2 * capacity):
            tags[m, 0] = -1
        received = (
            (aggs_up, z_up, row_index > 0),
            (aggs_down, z_down, row_index < lax.axis_size("rows") - 1),
        )
        for side, (other, other_z, there) in enumerate(received):

            @pl.when(there)
            def _(side=side, other=other, other_z=other_z):
                def scan(i, n):
                    a = other[1, i]
                    hit = lax.div(a, row_span) == row_index

                    @pl.when(hit)
                    def _():
                        tags[side * capacity + n, 0] = lax.rem(a, CR_DEV)
                        for s in range(4):
                            tags[side * capacity + n, 1 + s] = other_z[1, s, i]

                    return n + hit.astype(jnp.int32)

                lax.fori_loop(0, rows_here, scan, jnp.int32(0))

        for c in copies:
            c.wait()
        for side in range(2):
            for m in range(EARLY):
                a = tags[side * capacity + m, 0]

                @pl.when(a >= 0)
                def _(side=side, m=m, a=a):
                    for s in range(4):
                        t = a * COARSE_SLOTS + tags[side * capacity + m, 1 + s]
                        out[t] += got[side, m, s].astype(jnp.float32)

    def step(b, carry):
        first = b * TOGETHER
        lines = [g * block + first + n for n in range(TOGETHER)]
        for acc in accs:
            acc[...] = jnp.zeros_like(acc)
        for k in range(7):
            for n, i in enumerate(lines):
                v = cols[k, i]
                wide = jnp.concatenate([pall[v, 0], pall[v, 1]], axis=1)
                product = jnp.dot(a_ref[first + n, k], wide, preferred_element_type=jnp.float32)
                for l in range(2):
                    accs[n][slot[k, l, i]] += product[:, 128 * l : 128 * (l + 1)]
        for n, i in enumerate(lines):
            strip = jnp.concatenate([accs[n][s].astype(jnp.bfloat16) for s in range(4)], axis=1)
            for j in range(2):
                part = fold(pall[i, j], strip)
                base = lax.rem(aggs[j, i], CR_DEV) * COARSE_SLOTS
                here = lax.div(aggs[j, i], row_span) == row_index
                for s in range(4):
                    t = base + z[j, s, i]
                    if j:
                        t = jnp.where(here, t, TILES)
                    out[t] += part[:, 128 * s : 128 * (s + 1)]
        return carry

    lax.fori_loop(0, block // TOGETHER, step, 0)


def add_kernel(capacity, tags, up, down, c_in, c_out):
    g = pl.program_id(0)
    c_out[0] = c_in[...]
    for side, got in ((0, up), (1, down)):

        def step(m, carry, side=side, got=got):
            line = side * capacity + EARLY + m

            @pl.when(tags[line, 0] == g)
            def _():
                for s in range(4):
                    c_out[0, tags[line, 1 + s]] += got[m, s].astype(jnp.float32)

            return carry

        lax.fori_loop(0, got.shape[0], step, 0)


def local(a_tiles, a_cols, ap_slot, p_tiles, p_aggs, z_slot, send_rows):
    rows_here, _, tile, _ = a_tiles.shape
    a_cols, p_aggs = a_cols.T, p_aggs.T
    ap_slot, z_slot = ap_slot.transpose(1, 2, 0), z_slot.transpose(1, 2, 0)
    sends = send_rows.shape[2]
    capacity = max(2, rows_here // 8)
    late = capacity - EARLY
    smem = pl.BlockSpec(memory_space=SMEM)
    anys = pl.BlockSpec(memory_space=ANY)
    vmem = pl.BlockSpec(memory_space=VMEM)
    bf16 = jnp.bfloat16
    all_rows = rows_here + 4 * sends

    def boxes(n):
        return jax.ShapeDtypeStruct((n, 4, tile, tile), bf16)

    aggs_shape = jax.ShapeDtypeStruct(p_aggs.shape, jnp.int32)
    z_shape = jax.ShapeDtypeStruct(z_slot.shape, jnp.int32)
    ghosts, early_up, early_down, aggs_up, aggs_down, z_up, z_down, late_up, late_down = pl.pallas_call(
        lambda *r: front_kernel(capacity, *r),
        out_shape=[
            jax.ShapeDtypeStruct((4 * sends, 2, tile, tile), bf16),
            boxes(EARLY),
            boxes(EARLY),
            aggs_shape,
            aggs_shape,
            z_shape,
            z_shape,
            boxes(late),
            boxes(late),
        ],
        in_specs=[smem] * 4 + [anys] * 4,
        out_specs=[anys] * 7 + [vmem] * 2,
        scratch_shapes=[
            VMEM((all_rows, 2, tile, tile), bf16),
            VMEM((rows_here, 7, tile, tile), bf16),
            VMEM((4, sends, 2, tile, tile), bf16),
            VMEM((4 * sends, 2, tile, tile), bf16),
            VMEM((EARLY, 4, tile, tile), bf16),
            VMEM((EARLY, 4, tile, tile), bf16),
            VMEM((2 * GROUP, 7, tile, 2 * tile), jnp.float32),
            SMEM((2 * capacity,), jnp.int32),
            DMA((3,)),
            DMA((8 + 2 * EARLY,)),
            DMA((8 + 2 * EARLY,)),
        ],
        compiler_params=pltpu.CompilerParams(
            vmem_limit_bytes=VMEM_LIMIT, collective_id=0, has_side_effects=True
        ),
        cost_estimate=pl.CostEstimate(
            flops=2 * capacity * 36 * tile**3, bytes_accessed=25_000_000, transcendentals=0
        ),
    )(a_cols, ap_slot, p_aggs, send_rows, a_tiles, p_tiles, p_aggs, z_slot)
    up = passed_along(late_up, "rows", 1)
    down = passed_along(late_down, "rows", -1)
    block = math.gcd(rows_here, 8)
    coarse, tags = pl.pallas_call(
        lambda *r: main_kernel(capacity, *r),
        out_shape=[
            jax.ShapeDtypeStruct((TILES + 1, tile, tile), jnp.float32),
            jax.ShapeDtypeStruct((2 * capacity, 5), jnp.int32),
        ],
        grid=(rows_here // block,),
        in_specs=[smem] * 8
        + [pl.BlockSpec((block, 7, tile, tile), lambda g: (g, 0, 0, 0))]
        + [anys] * 4,
        out_specs=[pl.BlockSpec((TILES + 1, tile, tile), lambda g: (0, 0, 0)), smem],
        scratch_shapes=[
            VMEM((all_rows, 2, tile, tile), bf16),
            VMEM((2, EARLY, 4, tile, tile), bf16),
            DMA((4,)),
        ]
        + [VMEM((4, tile, tile), jnp.float32)] * TOGETHER,
        compiler_params=pltpu.CompilerParams(vmem_limit_bytes=MAIN_LIMIT),
        cost_estimate=pl.CostEstimate(
            flops=2 * rows_here * 22 * tile**3, bytes_accessed=26_000_000, transcendentals=0
        ),
    )(
        a_cols, ap_slot, p_aggs, z_slot, aggs_up, aggs_down, z_up, z_down,
        a_tiles, p_tiles, ghosts, early_up, early_down,
    )
    whole = pl.BlockSpec((late, 4, tile, tile), lambda g: (0, 0, 0, 0))
    return pl.pallas_call(
        lambda *r: add_kernel(capacity, *r),
        out_shape=jax.ShapeDtypeStruct((CR_DEV, COARSE_SLOTS, tile, tile), jnp.float32),
        grid=(CR_DEV,),
        in_specs=[
            smem,
            whole,
            whole,
            pl.BlockSpec((COARSE_SLOTS, tile, tile), lambda g: (g, 0, 0)),
        ],
        out_specs=pl.BlockSpec((1, COARSE_SLOTS, tile, tile), lambda g: (g, 0, 0, 0)),
        compiler_params=pltpu.CompilerParams(vmem_limit_bytes=ADD_LIMIT),
    )(tags, up, down, coarse)


def solution(mesh):
    spec = P(("rows", "cols"))
    return jax.shard_map(
        local,
        mesh=mesh,
        in_specs=(spec,) * 7,
        out_specs=spec,
        check_vma=False,
    )
```
